256 devices in a mesh: blk: 32 (over z, x_lo, core), uly: 8 (over y, x_hi).
Axes of the slice: x: 4 (x_hi: 2, x_lo: 2; x = x_hi * 2 + x_lo), y: 4, z: 8, core: 2. Of those that a mesh axis runs over, the one named last changes fastest.
Arguments:
- queries: bfloat16 [4096, 5120], P(('blk', 'uly')), may hold values from -120 to 120
- keys: bfloat16 [4096, 5120], P(('blk', 'uly')), may hold values from -6.5 to 6.5
- values: bfloat16 [4096, 5120], P(('blk', 'uly')), may hold values from -16 to 16
- block_lists: int32 [32, 12], P('blk'), may hold values from 0 to 31, as said below
- block_counts: int32 [32], P('blk'), may hold values from 4 to 12, as said below
- out_weight: bfloat16 [5120, 5120], P('uly', 'blk'), may hold values from -0.078125 to 0.078125
- out_bias: float32 [5120], replicated, may hold values from -1.8 to 1.8
- out_gate: float32 [5120], replicated, may hold values from 0.5 to 1.5
Outputs:
- branch_out: bfloat16 [4096, 5120], P(('blk', 'uly'))
The draws below stay inside these ranges and needn't reach their ends.
Inputs may be any that keep to these rules, and one draw needn't show every extreme that they name: `block_lists`: row i lists 12 distinct key-block numbers; its first entry is i itself; entries at slots block_counts[i] and beyond are ignored. `block_counts`: some query block uses all 12 slots.
All inputs are finite; a program needn't handle non-finite values.
Results may differ from the reference program's by a relative error of at most 0.015.
Values may be sent and summed in bfloat16 or wider, within the bound.
A program may use at most 128 MiB of HBM per device.

```python
import jax
import jax.numpy as jnp
from jax import lax

HEADS = 40
HEAD_DIM = 128
D = 5120
SHARD_TOK = 128
BLOCK = 128
FRAME_BLOCKS = 28
TOKENS = 4096
KEY_BLOCKS = 32
MOST_BLOCKS = 12
N_ULY = 8


def drawn_keys(key):
    base = jnp.clip(jax.random.normal(key, (TOKENS, D), jnp.float32), -6.0, 6.0)
    result = base
    result = jnp.clip(result, -6.5, 6.5)
    return result


def radial_table(key):
    block_ids = jnp.arange(KEY_BLOCKS, dtype=jnp.int32)
    frame_q = block_ids[:, None] // FRAME_BLOCKS
    frame_k = block_ids[None, :] // FRAME_BLOCKS
    place_q = block_ids[:, None] % FRAME_BLOCKS
    place_k = block_ids[None, :] % FRAME_BLOCKS
    frame_gap = jnp.abs(frame_q - frame_k)
    distance = 3 * frame_gap + jnp.abs(place_q - place_k)
    nearness = jnp.maximum(0, 20 - distance)
    nearness = jnp.where(place_q == place_k, jnp.maximum(nearness, 17 - frame_gap // 2), nearness)
    nearness = nearness + jax.random.randint(jax.random.fold_in(key, 21), (KEY_BLOCKS, KEY_BLOCKS), 0, 6)
    nearness = jnp.where(block_ids[:, None] == block_ids[None, :], 64, nearness)
    priority = nearness * 1024 + block_ids[None, :]
    lists = jax.lax.top_k(priority, MOST_BLOCKS)[1].astype(jnp.int32)
    counts = jax.random.randint(jax.random.fold_in(key, 22), (KEY_BLOCKS,), MOST_BLOCKS // 3, MOST_BLOCKS + 1)
    chosen = jax.random.randint(jax.random.fold_in(key, 23), (), 0, KEY_BLOCKS)
    counts = jnp.where(block_ids == chosen, MOST_BLOCKS, counts).astype(jnp.int32)
    return (lists, counts)


def draw_block_lists(key, part):
    return radial_table(key)[0]


def draw_block_counts(key, part):
    return radial_table(key)[1]


def draw_keys(key, part):
    result = drawn_keys(key)
    return result.astype(jnp.bfloat16)


def draw_queries(key, part):
    key = jax.random.fold_in(key, 3)
    own = 1.5 * jnp.clip(jax.random.normal(key, (TOKENS, D), jnp.float32), -6.0, 6.0)
    return own.astype(jnp.bfloat16)


def shard_levels(stream_key, extent, pieces, low, top_value):
    gain = 1.0
    for position, blocks in pieces:
        heights = jax.random.uniform(jax.random.fold_in(jax.random.fold_in(stream_key, 6), position), (blocks,), jnp.float32, low / len(pieces), top_value / len(pieces))
        gain = gain * jnp.repeat(jnp.exp(heights), extent[position] // blocks).reshape((-1,) + (1,) * (len(extent) - 1 - position))
    return gain


def bell_draw(key, shape, width, most, pieces=(), kind=jnp.bfloat16):
    values = width * jax.random.normal(key, shape, jnp.float32)
    if pieces:
        values = values * shard_levels(key, shape, pieces, -0.22, 0.18)
    return jnp.clip(values, -most, most).astype(kind)


def setup_inputs(seed: int = 0) -> dict:
    key_list = jax.random.split(jax.random.key(seed), 9)
    queries = draw_queries(jax.random.fold_in(key_list[8], 71), 0)
    keys = draw_keys(jax.random.fold_in(key_list[8], 71), 0)
    values = bell_draw(key_list[2], (TOKENS, D), 4.0, 16.0, ((0, 256),))
    block_lists = draw_block_lists(jax.random.fold_in(key_list[8], 71), 0)
    block_counts = draw_block_counts(jax.random.fold_in(key_list[8], 71), 0)
    out_weight = bell_draw(key_list[5], (D, D), D ** -0.5, 0.078125, ((0, 8), (1, 32)))
    out_bias = bell_draw(key_list[6], (D,), 0.3, 1.8, (), jnp.float32)
    out_gate = jnp.clip(jax.random.uniform(key_list[7], (D,), jnp.float32, 0.5, 1.5), 0.5, 1.5)
    return {"queries": queries, "keys": keys, "values": values, "block_lists": block_lists, "block_counts": block_counts, "out_weight": out_weight, "out_bias": out_bias, "out_gate": out_gate}


def block_table(block_lists, block_counts):
    listed = jnp.arange(MOST_BLOCKS)[None, :] < block_counts[:, None]
    matches = block_lists[:, :, None] == jnp.arange(KEY_BLOCKS, dtype=jnp.int32)[None, None, :]
    return jnp.any(matches & listed[:, :, None], axis=1)


def reference(queries, keys, values, block_lists, block_counts, out_weight, out_bias, out_gate):
    allowed = block_table(block_lists, block_counts)
    score_scale = HEAD_DIM ** -0.5

    def one_head(operands):
        q_head, k_head, v_head = operands

        def one_tile(first_row):
            q_tile = lax.dynamic_slice_in_dim(q_head, first_row, SHARD_TOK, 0)
            scores = jnp.dot(q_tile, k_head.T, preferred_element_type=jnp.float32) * score_scale
            tile_blocks = lax.dynamic_slice_in_dim(allowed, first_row // BLOCK, SHARD_TOK // BLOCK, 0)
            visible = jnp.repeat(jnp.repeat(tile_blocks, BLOCK, axis=0), BLOCK, axis=1)
            scores = jnp.where(visible, scores, -1e30)
            row_max = jnp.max(scores, axis=1, keepdims=True)
            probs = jnp.where(visible, jnp.exp(scores - row_max), 0.0)
            denom = jnp.sum(probs, axis=1, keepdims=True)
            weights = probs.astype(jnp.bfloat16)
            mixed = jnp.dot(weights, v_head, preferred_element_type=jnp.float32) / denom
            return mixed.astype(jnp.bfloat16)

        starts = jnp.arange(0, TOKENS, SHARD_TOK).astype(jnp.int32)
        return lax.map(one_tile, starts).reshape(TOKENS, HEAD_DIM)

    def split_heads(array):
        return array.reshape(TOKENS, HEADS, HEAD_DIM).transpose(1, 0, 2)

    attended = lax.map(one_head, (split_heads(queries), split_heads(keys), split_heads(values)))
    attended = attended.transpose(1, 0, 2).reshape(TOKENS, D)
    group = D // N_ULY
    summed = jnp.zeros((TOKENS, D), jnp.float32)
    for group_index in range(N_ULY):
        lower = group_index * group
        partial_value = jnp.dot(attended[:, lower:lower + group], out_weight[lower:lower + group], preferred_element_type=jnp.float32)
        rounded = lax.optimization_barrier(partial_value.astype(jnp.bfloat16))
        summed = summed + rounded.astype(jnp.float32)
    return (out_gate * (summed + out_bias)).astype(jnp.bfloat16)
```

```python
import functools

import jax
import jax.numpy as jnp
from jax import lax
from jax.experimental import pallas as pl
from jax.experimental.pallas import tpu as pltpu
from jax.sharding import PartitionSpec as P

MESH = pl.DeviceIdType.MESH
HEAD_DIM = 128
SLOTS = 12
DZ = (0, 1, 7, 2, 6, 3, 5, 4)
BF16 = jnp.bfloat16
F32 = jnp.float32


def coords():
    b = lax.axis_index("blk")
    u = lax.axis_index("uly")
    return (u % 2) * 2 + (b // 2) % 2, u // 2, b // 4, b % 2


def dev(x, y, z, c):
    return (z * 4 + (x % 2) * 2 + c, y * 2 + x // 2)


def wait_bytes(ref, sem):
    pltpu.make_async_copy(ref, ref, sem).wait()


def remote(src, dst, send, recv, device):
    return pltpu.make_async_remote_copy(
        src, dst, send, recv, device_id=device, device_id_type=MESH
    )


def greet(devices):
    bar = pltpu.get_barrier_semaphore()
    for d in devices:
        pl.semaphore_signal(bar, inc=1, device_id=d, device_id_type=MESH)
    pl.semaphore_wait(bar, len(devices))


def w_step(s, wbuf, w_send, w_recv):
    x, y, z, c = coords()
    out = []
    for way, sign in ((0, 1), (1, -1)):
        zb = (z - sign * (s - 1) + 8) % 8
        part = wbuf.at[zb] if s < 4 else wbuf.at[zb, pl.ds(400 * way, 400)]
        out.append(
            remote(part, part, w_send.at[way, s - 1], w_recv.at[way, s - 1],
                   dev(x, y, (z + sign + 8) % 8, c))
        )
    return out


def w_start(s, *refs):
    for cp in w_step(s, *refs):
        cp.start()


def w_wait(s, wbuf, w_send, w_recv):
    z = coords()[2]
    for way, sign in ((0, 1), (1, -1)):
        zb = (z - sign * s + 8) % 8
        part = wbuf.at[zb] if s < 4 else wbuf.at[zb, pl.ds(400 * way, 400)]
        wait_bytes(part, w_recv.at[way, s - 1])


def gather_kernel(
    q_ref, k_ref, v_ref, w_ref, kv, qbuf, wbuf,
    stage, recv_a, recv_b,
    send_sem, a_sem, b_sem, kv_send, kv_sem, kvb_send, kvb_sem,
    sib_send, sib_sem, q_send, qb_send, q_sem, w_send, w_recv,
):
    x, y, z, c = coords()
    half = z // 4
    row = z % 4
    wrefs = (wbuf, w_send, w_recv)

    for h in range(40):
        cols = pl.ds(h * HEAD_DIM, HEAD_DIM)
        stage[h, 0] = k_ref[:, cols]
        stage[h, 1] = v_ref[:, cols]
        stage[h, 2] = q_ref[:, cols]

    peers = [
        dev(x, (y + dy) % 4, (z + dz) % 8, c)
        for dz in range(8) for dy in range(4) if (dy, dz) != (0, 0)
    ]
    peers += [
        dev((x + dx) % 4, y, half * 4 + (z + dr) % 4, c) for dr in range(4) for dx in (1, 2, 3)
    ]
    peers.append(dev(x, y, z, 1 - c))
    greet(peers)

    for dz in DZ:
        zd = (z + dz) % 8

        def send_a(dy, _, dz=dz, zd=zd):
            yd = (y + dy) % 4
            head = yd * 10 + (zd // 4) * 5 + zd % 4
            remote(stage.at[head], recv_a.at[z, y], send_sem, a_sem.at[dz],
                   dev(x, yd, zd, c)).start()
            return 0

        if dz == 0:
            head = y * 10 + half * 5 + row
            pltpu.make_async_copy(stage.at[head], recv_a.at[z, y], a_sem.at[0]).start()
        lax.fori_loop(1 if dz == 0 else 0, 4, send_a, 0)
    for dh in range(2):
        hd = (half + dh) % 2

        def send_b(dy, _, hd=hd):
            yd = (y + dy) % 4
            remote(stage.at[yd * 10 + hd * 5 + 4], recv_b.at[half, y], send_sem, b_sem.at[0],
                   dev(x, yd, hd * 4 + row, c)).start()
            return 0

        if dh == 0:
            pltpu.make_async_copy(
                stage.at[y * 10 + half * 5 + 4], recv_b.at[half, y], b_sem.at[0]
            ).start()
        lax.fori_loop(1 if dh == 0 else 0, 4, send_b, 0)

    wbuf[z, 0:640] = w_ref[:, 0:128]
    wbuf[z, 640:800] = jnp.concatenate(
        [w_ref[160 * g : 160 * g + 160, 128:160] for g in range(4)], axis=1
    )
    w_start(1, *wrefs)

    def forward(dz):
        zs = (z - dz + 8) % 8
        wait_bytes(recv_a.at[zs], a_sem.at[dz])
        src = recv_a.at[zs, :, pl.ds(0, 2)]
        dst = kv.at[x, c, zs // 4, zs % 4]
        for dx in range(4):
            xd = (x + dx) % 4

            @pl.when(xd < 3)
            def _(dx=dx, xd=xd):
                if dx == 0:
                    pltpu.make_async_copy(src, dst, kv_sem.at[dz]).start()
                else:
                    remote(src, dst, kv_send.at[dx - 1, dz], kv_sem.at[dz],
                           dev(xd, y, z, c)).start()

        part = zs // 3
        qsrc = recv_a.at[zs, :, 2]
        qdst = qbuf.at[x, zs % 3]

        @pl.when(part == x)
        def _():
            pltpu.make_async_copy(qsrc, qdst, q_sem.at[0]).start()

        @pl.when(part != x)
        def _():
            remote(qsrc, qdst, q_send.at[dz], q_sem.at[0], dev(part, y, z, c)).start()

    def to_sibling(dz):
        zs = (z - dz + 8) % 8

        @pl.when(x < 3)
        def _():
            got = kv.at[:, c, zs // 4, zs % 4]
            wait_bytes(got, kv_sem.at[dz])
            remote(got, got, sib_send.at[dz], sib_sem.at[dz], dev(x, y, z, 1 - c)).start()

    for i, dz in enumerate(DZ):
        forward(dz)
        if i >= 2:
            to_sibling(DZ[i - 2])
        if i == 3:
            w_wait(1, *wrefs)
            w_start(2, *wrefs)

    wait_bytes(recv_b, b_sem.at[0])
    bsrc = recv_b.at[:, :, pl.ds(0, 2)]
    bdst = kv.at[x, c, :, row]
    for dr in range(4):
        rd = (z + dr) % 4
        if dr == 0:
            @pl.when(x == 3)
            def _():
                pltpu.make_async_copy(bsrc, bdst, kvb_sem.at[0]).start()

            @pl.when(x != 3)
            def _():
                remote(bsrc, bdst, kvb_send.at[0], kvb_sem.at[0], dev(3, y, z, c)).start()
        else:
            remote(bsrc, bdst, kvb_send.at[dr], kvb_sem.at[dr],
                   dev(3, y, half * 4 + rd, c)).start()
    qsrc_b = recv_b.at[:, :, 2]
    qdst_b = qbuf.at[x, pl.ds(0, 2)]

    @pl.when(x == 3)
    def _():
        pltpu.make_async_copy(qsrc_b, qdst_b, q_sem.at[0]).start()

    @pl.when(x != 3)
    def _():
        remote(qsrc_b, qdst_b, qb_send.at[0], q_sem.at[0], dev(3, y, z, c)).start()

    to_sibling(DZ[6])
    w_wait(2, *wrefs)
    w_start(3, *wrefs)
    to_sibling(DZ[7])

    @pl.when(x == 3)
    def _():
        for dr in range(4):
            got = kv.at[:, c, :, (z - dr + 4) % 4]
            wait_bytes(got, kvb_sem.at[dr])
            remote(got, got, sib_send.at[dr], sib_sem.at[dr], dev(x, y, z, 1 - c)).start()

    @pl.when(x < 2)
    def _():
        wait_bytes(qbuf, q_sem.at[0])

    @pl.when(x >= 2)
    def _():
        wait_bytes(qbuf.at[:, pl.ds(0, 2)], q_sem.at[0])

    @pl.when(x < 3)
    def _():
        for dz in DZ:
            zs = (z - dz + 8) % 8
            wait_bytes(kv.at[:, 1 - c, zs // 4, zs % 4], sib_sem.at[dz])
            wait_bytes(kv.at[:, c, zs // 4, zs % 4], sib_send.at[dz])

    @pl.when(x == 3)
    def _():
        for dr in range(4):
            rs = (z - dr + 4) % 4
            wait_bytes(kv.at[:, 1 - c, :, rs], sib_sem.at[dr])
            wait_bytes(kv.at[:, c, :, rs], sib_send.at[dr])

    w_wait(3, *wrefs)
    w_start(4, *wrefs)
    wait_bytes(stage.at[pl.ds(0, 38)], send_sem)
    for dz in range(8):
        zs = (z - dz + 8) % 8
        for dx in (1, 2, 3):
            @pl.when((x + dx) % 4 < 3)
            def _(dx=dx):
                wait_bytes(recv_a.at[zs, :, pl.ds(0, 2)], kv_send.at[dx - 1, dz])

        @pl.when(zs // 3 != x)
        def _():
            wait_bytes(recv_a.at[zs, :, 2], q_send.at[dz])
    for dr in range(4):
        if dr == 0:
            @pl.when(x != 3)
            def _():
                wait_bytes(bsrc, kvb_send.at[0])
                wait_bytes(qsrc_b, qb_send.at[0])
        else:
            wait_bytes(bsrc, kvb_send.at[dr])
    w_wait(4, *wrefs)
    for s in (1, 2, 3, 4):
        for cp in w_step(s, *wrefs):
            cp.wait_send()


def attend_kernel(lists, kv, qbuf, att, kg, vg, sc, pr):
    x, y, z, c = coords()
    scale = float(HEAD_DIM ** -0.5 * 1.4426950408889634)

    def item(i, _):
        zi = i // 2
        xl = i % 2
        zq = jnp.where(x < 3, 3 * x + zi, zi * 4 + z % 4)
        blk = zq * 4 + xl * 2 + c
        count = lists[blk, SLOTS]
        q = jnp.concatenate(
            [qbuf[xl, zi].reshape(64, 128), qbuf[xl + 2, zi].reshape(64, 128)], axis=0
        )
        top = None
        for s in range(SLOTS):
            kb = lists[blk, s]
            kz = kb // 4
            for xh in range(2):
                got = kv.at[(kb // 2) % 2 + 2 * xh, kb % 2, kz // 4, kz % 4]
                rows = pl.ds(s * 128 + xh * 64, 64)
                kg[rows, :] = got[:, 0].reshape(64, 128)
                vg[rows, :] = got[:, 1].reshape(64, 128)
            part = lax.dot_general(
                q, kg[s * 128 : s * 128 + 128, :], (((1,), (1,)), ((), ())),
                preferred_element_type=F32,
            )
            part = jnp.where(s < count, part, -1e30)
            sc[s] = part
            top = part if top is None else jnp.maximum(top, part)
        top = jnp.max(top, axis=1, keepdims=True)
        den = jnp.zeros((128, 128), F32)
        for s in range(SLOTS):
            p = jnp.exp2((sc[s] - top) * scale)
            den = den + p
            pr[:, s * 128 : s * 128 + 128] = p.astype(BF16)
        mixed = jnp.dot(pr[...], vg[...], preferred_element_type=F32)
        den = jnp.sum(den, axis=1, keepdims=True)
        att[zi, xl] = (mixed / den).astype(BF16)
        return 0

    lax.fori_loop(0, jnp.where(x < 2, 6, 4), item, 0)


def project_kernel(
    att, wbuf, bias, gate, out,
    att_t, acat, wrest, psend, precv, rsum, rrecv,
    c_send, c_recv, s_send, s_recv, rs_send, rs_recv, f_send, f_recv,
):
    x, y, z, c = coords()
    half = z // 4
    xh = x // 2
    xl = x % 2
    peers = [
        dev((x + dx) % 4, y, (z + dz) % 8, c)
        for dz in range(8) for dx in range(4) if (dx, dz) != (0, 0)
    ]
    peers += [
        dev((x + 2 * dxh) % 4, (y + dy) % 4, z, c) for dy in (1, 2, 3) for dxh in range(2)
    ]
    other = xh * 2 + 1 - xl
    peers += [dev(x, y, z, 1 - c), dev(other, y, z, 1 - c)]
    greet(peers)

    j_mine = jnp.where(x < 3, z % 4, 4)

    def c_copies(act):
        for zi in range(3):
            zt = jnp.where(x < 3, 3 * x + zi, zi * 4 + z % 4) % 8
            for x2 in range(2):
                xd = half * 2 + x2
                here = (xd == x) & (zt == z)
                live = (x < 2) if zi == 2 else (x < 4)

                @pl.when(live & jnp.logical_not(here))
                def _(zi=zi, zt=zt, x2=x2, xd=xd):
                    act(zi, zt, x2, xd, False)

                @pl.when(live & here)
                def _(zi=zi, zt=zt, x2=x2, xd=xd):
                    act(zi, zt, x2, xd, True)

    def c_start(zi, zt, x2, xd, here):
        dst = att_t.at[j_mine, c]
        if here:
            pltpu.make_async_copy(att.at[zi], dst, c_recv.at[j_mine]).start()
        else:
            remote(att.at[zi], dst, c_send.at[zi, x2], c_recv.at[j_mine],
                   dev(xd, y, zt, c)).start()

    c_copies(c_start)

    for g in range(4):
        wrest[160 * g : 160 * g + 160, :] = jnp.concatenate(
            [wbuf[zz, 640:800, 32 * g : 32 * g + 32] for zz in range(8)], axis=1
        )

    for j in range(5):
        got = att_t.at[j, c]
        wait_bytes(got, c_recv.at[j])
        remote(got, got, s_send.at[j], s_recv.at[j], dev(x, y, z, 1 - c)).start()
    for j in range(5):
        wait_bytes(att_t.at[j, 1 - c], s_recv.at[j])
        for c2 in range(2):
            for x2 in range(2):
                r0 = (c2 * 2 + x2) * 128
                acat[r0 : r0 + 128, j * 128 : j * 128 + 128] = att_t[j, c2, x2]

    def rs_copy(n, dxh, dy):
        xd = (x + 2 * dxh) % 4
        yd = (y + dy) % 4
        return remote(psend.at[n, xd // 2 * 4 + yd], precv.at[n, xh * 4 + y],
                      rs_send.at[n], rs_recv.at[n], dev(xd, yd, z, c))

    order = [(1, 2), (0, 2), (1, 1), (1, 3), (1, 0), (0, 1), (0, 3)]
    for n in range(5):
        if n < 4:
            wn = jnp.concatenate([wbuf[2 * n, 0:640], wbuf[2 * n + 1, 0:640]], axis=1)
        else:
            wn = wrest[...]
        r = jnp.dot(acat[...], wn, preferred_element_type=F32).astype(BF16)
        for c2 in range(2):
            for x2 in range(2):
                r0 = (c2 * 2 + x2) * 128
                psend[n, :, c2, x2] = r[r0 : r0 + 128].reshape(8, 16, 256)
        for dxh, dy in order:
            rs_copy(n, dxh, dy).start()

    for n in range(5):
        wait_bytes(precv.at[n, pl.ds(0, 7)], rs_recv.at[n])
        mine = xh * 4 + y
        total = psend[n, mine].astype(F32)
        for d in range(1, 8):
            total = total + precv[n, (mine + d) % 8].astype(F32)
        rsum[:, :, n] = total.astype(BF16)

    finals = []
    for i, (dxl, dc) in enumerate(((1, 1), (1, 0), (0, 1))):
        xl2 = (xl + dxl) % 2
        c2 = (c + dc) % 2
        cp = remote(rsum.at[c2, xl2], rrecv.at[xl, c], f_send.at[i], f_recv.at[i],
                    dev(xh * 2 + xl2, y, z, c2))
        cp.start()
        finals.append(cp)
    rrecv[xl, c] = rsum[c, xl]
    for cp in finals:
        cp.wait_recv()

    lane = lax.broadcasted_iota(jnp.int32, (16, 128), 1)

    def glue(parts, shifts):
        out = None
        edge = 0
        for p, (shift, width) in zip(parts, shifts):
            moved = pltpu.roll(p, shift % 128, 1) if shift % 128 else p
            out = moved if out is None else jnp.where(lane >= edge, moved, out)
            edge += width
        return out

    for zz in range(8):
        m = []
        r = []
        for i in range(4):
            got = rrecv[i // 2, i % 2, zz // 2, :, (zz % 2) * 128 : (zz % 2) * 128 + 128]
            m.append(got.astype(F32))
            lo = (zz // 4) * 128
            got = rrecv[i // 2, i % 2, 4, :, lo : lo + 128].astype(F32)
            r.append(got)
        o = (32 * zz) % 128
        tiles = [
            m[0],
            glue([r[0], m[1]], [(-o, 32), (32, 96)]),
            glue([m[1], r[1], m[2]], [(32, 32), (32 - o, 32), (64, 64)]),
            glue([m[2], r[2], m[3]], [(64, 64), (64 - o, 32), (96, 32)]),
            glue([m[3], r[3]], [(96, 96), (96 - o, 32)]),
        ]
        for t in range(5):
            cols = slice(zz * 640 + t * 128, zz * 640 + t * 128 + 128)
            out[:, cols] = (gate[:, cols] * (tiles[t] + bias[:, cols])).astype(BF16)

    def c_done(zi, zt, x2, xd, here):
        if not here:
            wait_bytes(att.at[zi], c_send.at[zi, x2])

    c_copies(c_done)
    for j in range(5):
        wait_bytes(att_t.at[j, c], s_send.at[j])
    for n in range(5):
        wait_bytes(psend.at[n, pl.ds(0, 7)], rs_send.at[n])
    for cp in finals:
        cp.wait_send()


VM = pl.BlockSpec(memory_space=pltpu.VMEM)
SM = pl.BlockSpec(memory_space=pltpu.SMEM)
DMA = pltpu.SemaphoreType.DMA
LIMIT = 48 * 2**20


def body(queries, keys, values, block_lists, block_counts, out_weight, out_bias, out_gate):
    local = jnp.concatenate(
        [block_lists, block_counts[:, None], jnp.zeros((1, 3), jnp.int32)], axis=1
    )
    lists = lax.all_gather(local, "blk", axis=0, tiled=True)
    shape = jax.ShapeDtypeStruct
    kv, qbuf, wbuf = pl.pallas_call(
        gather_kernel,
        out_shape=(
            shape((4, 2, 2, 4, 4, 2, 16, 128), BF16),
            shape((4, 3, 4, 16, 128), BF16),
            shape((8, 800, 128), BF16),
        ),
        in_specs=[VM] * 4,
        out_specs=(VM, VM, VM),
        scratch_shapes=[
            pltpu.VMEM((40, 3, 16, 128), BF16),
            pltpu.VMEM((8, 4, 3, 16, 128), BF16),
            pltpu.VMEM((2, 4, 3, 16, 128), BF16),
            DMA, DMA((8,)), DMA((1,)), DMA((3, 8)), DMA((8,)), DMA((4,)), DMA((4,)),
            DMA((8,)), DMA((8,)), DMA((8,)), DMA((1,)), DMA((1,)), DMA((2, 4)), DMA((2, 4)),
        ],
        compiler_params=pltpu.CompilerParams(
            collective_id=0, has_side_effects=True, vmem_limit_bytes=LIMIT
        ),
        name="gather",
    )(queries, keys, values, out_weight)
    att = pl.pallas_call(
        attend_kernel,
        out_shape=shape((3, 2, 128, 128), BF16),
        in_specs=[SM, VM, VM],
        out_specs=VM,
        scratch_shapes=[
            pltpu.VMEM((SLOTS * 128, 128), BF16),
            pltpu.VMEM((SLOTS * 128, 128), BF16),
            pltpu.VMEM((SLOTS, 128, 128), F32),
            pltpu.VMEM((128, SLOTS * 128), BF16),
        ],
        compiler_params=pltpu.CompilerParams(vmem_limit_bytes=LIMIT),
        name="attend",
    )(lists, kv, qbuf)
    return pl.pallas_call(
        project_kernel,
        out_shape=shape((16, 5120), BF16),
        in_specs=[VM] * 4,
        out_specs=VM,
        scratch_shapes=[
            pltpu.VMEM((5, 2, 2, 128, 128), BF16),
            pltpu.VMEM((512, 640), BF16),
            pltpu.VMEM((640, 256), BF16),
            pltpu.VMEM((5, 8, 2, 2, 16, 256), BF16),
            pltpu.VMEM((5, 8, 2, 2, 16, 256), BF16),
            pltpu.VMEM((2, 2, 5, 16, 256), BF16),
            pltpu.VMEM((2, 2, 5, 16, 256), BF16),
            DMA((3, 2)), DMA((5,)), DMA((5,)), DMA((5,)), DMA((5,)), DMA((5,)),
            DMA((3,)), DMA((3,)),
        ],
        compiler_params=pltpu.CompilerParams(
            collective_id=1, has_side_effects=True, vmem_limit_bytes=LIMIT
        ),
        name="project",
    )(att, wbuf, out_bias.reshape(1, -1), out_gate.reshape(1, -1))


def solution(mesh):
    in_specs = (
        P(("blk", "uly"), None),
        P(("blk", "uly"), None),
        P(("blk", "uly"), None),
        P("blk", None),
        P("blk"),
        P("uly", "blk"),
        P(),
        P(),
    )
    out_specs = P(("blk", "uly"), None)
    return jax.shard_map(body, mesh=mesh, in_specs=in_specs, out_specs=out_specs, check_vma=False)
```

```python
import functools

import jax
import jax.numpy as jnp
from jax import lax
from jax.experimental import pallas as pl
from jax.experimental.pallas import tpu as pltpu
from jax.sharding import PartitionSpec as P

MESH = pl.DeviceIdType.MESH
HEAD_DIM = 128
SLOTS = 12
DZ = (0, 1, 7, 2, 6, 3, 5, 4)
BF16 = jnp.bfloat16
F32 = jnp.float32


def coords():
    b = lax.axis_index("blk")
    u = lax.axis_index("uly")
    return (u % 2) * 2 + (b // 2) % 2, u // 2, b // 4, b % 2


def dev(x, y, z, c):
    return (z * 4 + (x % 2) * 2 + c, y * 2 + x // 2)


def wait_bytes(ref, sem):
    pltpu.make_async_copy(ref, ref, sem).wait()


def remote(src, dst, send, recv, device):
    return pltpu.make_async_remote_copy(
        src, dst, send, recv, device_id=device, device_id_type=MESH
    )


def mega_kernel(
    q_ref, k_ref, v_ref, lists_ref, counts_ref, w_ref, bias, gate, out,
    stage, recv_a, recv_b, kv, qbuf, lbuf, lsm, kg, vg, sc, pr, att, att_t,
    wsrc, wbuf, acat, wrest, psend, precv, rsum, rrecv,
    send_sem, a_sem, b_sem, kv_send, kv_sem, kvb_send, kvb_sem,
    sib_send, sib_sem, q_send, qb_send, q_sem, l_send, l_recv, l_sem,
    wx_send, wx_recv, w_send, w_recv, ws_send, ws_recv,
    c_send, c_recv, r_send, r_recv, rs_send, rs_recv, f_send, f_recv,
):
    x, y, z, c = coords()
    half = z // 4
    row = z % 4
    xh = x // 2
    xl = x % 2

    for h in range(40):
        cols = pl.ds(h * HEAD_DIM, HEAD_DIM)
        stage[h, 0] = k_ref[:, cols]
        stage[h, 1] = v_ref[:, cols]
        stage[h, 2] = q_ref[:, cols]
    lbuf[xl, z] = jnp.full((1, 128), counts_ref[0], jnp.int32)
    lbuf[xl, z, :, 0:SLOTS] = lists_ref[...]

    peers = [
        dev(x, (y + dy) % 4, (z + dz) % 8, c)
        for dz in range(8) for dy in range(4) if (dy, dz) != (0, 0)
    ]
    peers += [dev((x + dx) % 4, y, (z + dz) % 8, c) for dz in range(8) for dx in (1, 2, 3)]
    peers += [dev(x, y, z, 1 - c), dev((x + 2) % 4, y, z, 1 - c)]
    bar = pltpu.get_barrier_semaphore()
    for d in peers:
        pl.semaphore_signal(bar, inc=1, device_id=d, device_id_type=MESH)
    wsrc[0:640] = w_ref[:, 0:128]
    wsrc[640:800] = jnp.concatenate(
        [w_ref[160 * g : 160 * g + 160, 128:160] for g in range(4)], axis=1
    )
    pl.semaphore_wait(bar, len(peers))

    for dz in range(1, 8):
        remote(lbuf.at[xl, z], lbuf.at[xl, z], l_send.at[dz], l_recv.at[dz],
               dev(x, y, (z + dz) % 8, c)).start()

    def stage1_a(dz):
        zd = (z + dz) % 8

        def send_a(dy, _):
            yd = (y + dy) % 4
            head = yd * 10 + (zd // 4) * 5 + zd % 4
            remote(stage.at[head], recv_a.at[z, y], send_sem, a_sem.at[dz],
                   dev(x, yd, zd, c)).start()
            return 0

        if dz == 0:
            head = y * 10 + half * 5 + row
            pltpu.make_async_copy(stage.at[head], recv_a.at[z, y], a_sem.at[0]).start()
        lax.fori_loop(1 if dz == 0 else 0, 4, send_a, 0)

    def stage1_b():
        for dh in range(2):
            hd = (half + dh) % 2

            def send_b(dy, _, hd=hd):
                yd = (y + dy) % 4
                remote(stage.at[yd * 10 + hd * 5 + 4], recv_b.at[half, y], send_sem,
                       b_sem.at[0], dev(x, yd, hd * 4 + row, c)).start()
                return 0

            if dh == 0:
                pltpu.make_async_copy(
                    stage.at[y * 10 + half * 5 + 4], recv_b.at[half, y], b_sem.at[0]
                ).start()
            lax.fori_loop(1 if dh == 0 else 0, 4, send_b, 0)

    for dz in DZ[:B_AT]:
        stage1_a(dz)
    stage1_b()
    for dz in DZ[B_AT:]:
        stage1_a(dz)

    @pl.when(xh == c)
    def _():
        pltpu.make_async_copy(wsrc, wbuf.at[c, z], wx_recv.at[0]).start()

    @pl.when(xh != c)
    def _():
        remote(wsrc, wbuf.at[xh, z], wx_send.at[0], wx_recv.at[0],
               dev((x + 2) % 4, y, z, 1 - c)).start()

    def w_part(zb, s, way):
        return wbuf.at[c, zb] if s < 4 else wbuf.at[c, zb, pl.ds(400 * way, 400)]

    def w_copies(s):
        got = []
        for way, sign in ((0, 1), (1, -1)):
            part = w_part((z - sign * (s - 1) + 8) % 8, s, way)
            got.append(remote(part, part, w_send.at[way, s - 1], w_recv.at[way, s - 1],
                              dev(x, y, (z + sign + 8) % 8, c)))
        return got

    def w_sib(zb, k):
        part = wbuf.at[c, zb]
        return remote(part, part, ws_send.at[k], ws_recv.at[k], dev(x, y, z, 1 - c))

    def w_start(s):
        if s == 1:
            wait_bytes(wbuf.at[c, z], wx_recv.at[0])
        else:
            for way, sign in ((0, 1), (1, -1)):
                part = w_part((z - sign * (s - 1) + 8) % 8, s - 1, way)
                wait_bytes(part, w_recv.at[way, s - 2])
        if s < 5:
            for cp in w_copies(s):
                cp.start()
        if s == 1:
            w_sib(z, 0).start()
        elif s < 5:
            w_sib((z - s + 9) % 8, 2 * s - 3).start()
            w_sib((z + s - 1) % 8, 2 * s - 2).start()
        else:
            w_sib((z + 4) % 8, 7).start()

    def w_order():
        got = [(0, z)]
        for s in (2, 3, 4):
            got += [(2 * s - 3, (z - s + 9) % 8), (2 * s - 2, (z + s - 1) % 8)]
        return got + [(7, (z + 4) % 8)]

    def forward(dz):
        zs = (z - dz + 8) % 8
        wait_bytes(recv_a.at[zs], a_sem.at[dz])
        src = recv_a.at[zs, :, pl.ds(0, 2)]
        dst = kv.at[x, c, zs // 4, zs % 4]
        for dx in (2, 1, 3, 0):
            xd = (x + dx) % 4

            @pl.when(xd < 3)
            def _(dx=dx, xd=xd):
                if dx == 0:
                    pltpu.make_async_copy(src, dst, kv_sem.at[dz]).start()
                else:
                    remote(src, dst, kv_send.at[dx - 1, dz], kv_sem.at[dz],
                           dev(xd, y, z, c)).start()

        part = zs // 3
        qsrc = recv_a.at[zs, :, 2]
        qdst = qbuf.at[x, zs % 3]

        @pl.when(part == x)
        def _():
            pltpu.make_async_copy(qsrc, qdst, q_sem.at[0]).start()

        @pl.when(part != x)
        def _():
            remote(qsrc, qdst, q_send.at[dz], q_sem.at[0], dev(part, y, z, c)).start()

    def to_sibling(dz):
        zs = (z - dz + 8) % 8

        @pl.when(x < 3)
        def _():
            got = kv.at[:, c, zs // 4, zs % 4]
            wait_bytes(got, kv_sem.at[dz])
            remote(got, got, sib_send.at[dz], sib_sem.at[dz], dev(x, y, z, 1 - c)).start()

    bsrc = recv_b.at[:, :, pl.ds(0, 2)]
    bdst = kv.at[x, c, :, row]
    qsrc_b = recv_b.at[:, :, 2]
    qdst_b = qbuf.at[x, pl.ds(0, 2)]

    def forward_b():
        wait_bytes(recv_b, b_sem.at[0])
        for dr in (2, 1, 3, 0):
            rd = (z + dr) % 4
            if dr == 0:
                @pl.when(x == 3)
                def _():
                    pltpu.make_async_copy(bsrc, bdst, kvb_sem.at[0]).start()
                    pltpu.make_async_copy(qsrc_b, qdst_b, q_sem.at[0]).start()

                @pl.when(x != 3)
                def _():
                    remote(bsrc, bdst, kvb_send.at[0], kvb_sem.at[0], dev(3, y, z, c)).start()
                    remote(qsrc_b, qdst_b, qb_send.at[0], q_sem.at[0], dev(3, y, z, c)).start()
            else:
                remote(bsrc, bdst, kvb_send.at[dr], kvb_sem.at[dr],
                       dev(3, y, half * 4 + rd, c)).start()

    def forward_lists():
        for dz in range(1, 8):
            wait_bytes(lbuf.at[xl, (z - dz + 8) % 8], l_recv.at[dz])
        remote(lbuf.at[xl], lbuf.at[xl], l_send.at[0], l_recv.at[0],
               dev(xh * 2 + 1 - xl, y, z, c)).start()

    def place_lists():
        wait_bytes(lbuf.at[1 - xl], l_recv.at[0])
        cp = pltpu.make_async_copy(lbuf, lsm, l_sem.at[0])
        cp.start()
        cp.wait()

    for i, dz in enumerate(DZ):
        forward(dz)
        if i >= 2:
            to_sibling(DZ[i - 2])
        if i == B_FWD:
            forward_b()
        if i == W1_AT:
            w_start(1)
        if i == W2_AT:
            w_start(2)
    forward_lists()
    to_sibling(DZ[6])
    to_sibling(DZ[7])

    @pl.when(x == 3)
    def _():
        for dr in range(4):
            got = kv.at[:, c, :, (z - dr + 4) % 4]
            wait_bytes(got, kvb_sem.at[dr])
            remote(got, got, sib_send.at[dr], sib_sem.at[dr], dev(x, y, z, 1 - c)).start()

    place_lists()

    @pl.when(x < 2)
    def _():
        wait_bytes(qbuf, q_sem.at[0])

    @pl.when(x >= 2)
    def _():
        wait_bytes(qbuf.at[:, pl.ds(0, 2)], q_sem.at[0])

    @pl.when(x < 3)
    def _():
        for dz in DZ:
            zs = (z - dz + 8) % 8
            wait_bytes(kv.at[:, 1 - c, zs // 4, zs % 4], sib_sem.at[dz])

    @pl.when(x == 3)
    def _():
        for dr in range(4):
            wait_bytes(kv.at[:, 1 - c, :, (z - dr + 4) % 4], sib_sem.at[dr])

    if W2_AT >= 8:
        w_start(2)

    scale = float(HEAD_DIM ** -0.5 * 1.4426950408889634)
    j_mine = jnp.where(x < 3, row, 4)
    h_mine = half * 5 + j_mine
    slot_mine = jnp.where(x < 3, half, 2)
    n_zi = jnp.where(x < 2, 3, 2)

    def c_place(zi, l):
        zt = jnp.where(x < 3, 3 * x + zi, zi * 4 + row) % 8
        xd = jnp.where(x < 3, row, half * 2 + l)
        return zt, xd, (zt == z) & (xd == x)

    def item(zi, l):
        zq = jnp.where(x < 3, 3 * x + zi, zi * 4 + row) % 8
        count = lsm[l, zq, 0, SLOTS]
        q = jnp.concatenate(
            [qbuf[l, zi].reshape(64, 128), qbuf[l + 2, zi].reshape(64, 128)], axis=0
        )
        top = None
        for s in range(SLOTS):
            kb = lsm[l, zq, 0, s]
            kz = kb // 4
            for a in range(2):
                rows = pl.ds(s * 128 + a * 64, 64)
                got = kv[(kb // 2) % 2 + 2 * a, kb % 2, kz // 4, kz % 4]
                kg[rows, :] = got[:, 0].reshape(64, 128)
                vg[rows, :] = got[:, 1].reshape(64, 128)
            part = lax.dot_general(
                q, kg[s * 128 : s * 128 + 128, :], (((1,), (1,)), ((), ())),
                preferred_element_type=F32,
            )
            part = jnp.where(s < count, part, -1e30)
            sc[s] = part
            top = part if top is None else jnp.maximum(top, part)
        top = jnp.max(top, axis=1, keepdims=True)
        den = jnp.zeros((128, 128), F32)
        for s in range(SLOTS):
            p = jnp.exp2((sc[s] - top) * scale)
            den = den + p
            pr[:, s * 128 : s * 128 + 128] = p.astype(BF16)
        mixed = jnp.dot(pr[...], vg[...], preferred_element_type=F32)
        den = jnp.sum(den, axis=1, keepdims=True)
        att[zi, l] = (mixed / den).astype(BF16)
        zt, xd, here = c_place(zi, l)
        src = att.at[zi, l]
        dst = att_t.at[l, h_mine]
        sem = c_recv.at[l, slot_mine]

        @pl.when(here)
        def _():
            pltpu.make_async_copy(src, dst, sem).start()

        @pl.when(jnp.logical_not(here))
        def _():
            remote(src, dst, c_send.at[l, zi], sem, dev(xd, y, zt, c)).start()

    def items(l):
        def step(zi, _):
            item(zi, l)
            return 0

        lax.fori_loop(0, n_zi, step, 0)

    def relay_one(l, h, k):
        got = att_t.at[l, h]
        wait_bytes(got, c_recv.at[l, k])
        for dx in (2, 1, 3):
            remote(got, got, r_send.at[l, k, dx - 1], r_recv.at[l, h],
                   dev((x + dx) % 4, y, z, c)).start()

    def relay(l):
        relay_one(l, x, 0)
        relay_one(l, 5 + x, 1)

        @pl.when(xl == l)
        def _():
            relay_one(l, xh * 5 + 4, 2)

    def relayed(l):
        for h in range(10):
            source = h % 5 if h % 5 < 4 else (h // 5) * 2 + l

            @pl.when(x != source)
            def _(h=h):
                wait_bytes(att_t.at[l, h], r_recv.at[l, h])

            acat[:, h * 128 : h * 128 + 128] = att_t[l, h]

    def rs_copy(l, g, dy):
        yd = (y + dy) % 4
        cols = pl.ds(0, 3) if g == 0 else pl.ds(3, 2)
        return remote(psend.at[l, yd, cols], precv.at[l, y, cols], rs_send.at[l, g, dy - 1],
                      rs_recv.at[l, g], dev(x, yd, z, c))

    def project(l):
        for n in range(5):
            if n < 4:
                wn = [
                    jnp.concatenate([wbuf[k, 2 * n, 0:640], wbuf[k, 2 * n + 1, 0:640]], axis=1)
                    for k in range(2)
                ]
            else:
                wn = [wrest[0], wrest[1]]
            r = jnp.dot(acat[:, 0:640], wn[0], preferred_element_type=F32)
            r = r + jnp.dot(acat[:, 640:1280], wn[1], preferred_element_type=F32)
            r = r.astype(BF16).reshape(2, 4, 16, 256)
            for yy in range(4):
                for a in range(2):
                    psend[l, yy, n, a] = r[a, yy]
            if n in (2, 4):
                for dy in (2, 1, 3):
                    rs_copy(l, n // 4, dy).start()

    def f_place(l, a):
        return a * 2 + l

    def reduce(l):
        for g in range(2):
            cols = slice(0, 3) if g == 0 else slice(3, 5)
            wait_bytes(precv.at[l, pl.ds(0, 3), pl.ds(0, 3) if g == 0 else pl.ds(3, 2)],
                       rs_recv.at[l, g])
            total = psend[l, y, cols].astype(F32)
            for d in (1, 2, 3):
                total = total + precv[l, (y + d) % 4, cols].astype(F32)
            total = total.astype(BF16)
            for a in range(2):
                rsum[l, a, cols] = total[:, a]
        for a in range(2):
            xd = f_place(l, a)

            @pl.when(xd == x)
            def _(a=a):
                rrecv[x] = rsum[l, a]

            @pl.when(xd != x)
            def _(a=a, xd=xd):
                remote(rsum.at[l, a], rrecv.at[x], f_send.at[l, a], f_recv.at[x],
                       dev(xd, y, z, c)).start()

    items(0)
    w_start(3)
    items(1)
    relay(0)
    w_start(4)
    relay(1)
    w_start(5)
    for k, zb in w_order():
        wait_bytes(wbuf.at[1 - c, zb], ws_recv.at[k])
    for k in range(2):
        for g in range(4):
            wrest[k, 160 * g : 160 * g + 160, :] = jnp.concatenate(
                [wbuf[k, zz, 640:800, 32 * g : 32 * g + 32] for zz in range(8)], axis=1
            )
    relayed(0)
    project(0)
    relayed(1)
    project(1)
    reduce(0)
    reduce(1)

    for d in (1, 2, 3):
        xs = (x + d) % 4
        wait_bytes(rrecv.at[xs], f_recv.at[xs])
    lane = lax.broadcasted_iota(jnp.int32, (16, 128), 1)

    def glue(parts, shifts):
        made = None
        edge = 0
        for p, (shift, width) in zip(parts, shifts):
            moved = pltpu.roll(p, shift % 128, 1) if shift % 128 else p
            made = moved if made is None else jnp.where(lane >= edge, moved, made)
            edge += width
        return made

    for zz in range(8):
        m = []
        r = []
        lo = (zz // 4) * 128
        for i in range(4):
            xs = (i % 2) * 2 + i // 2
            got = rrecv[xs, zz // 2, :, (zz % 2) * 128 : (zz % 2) * 128 + 128]
            m.append(got.astype(F32))
            r.append(rrecv[xs, 4, :, lo : lo + 128].astype(F32))
        o = (32 * zz) % 128
        tiles = [
            m[0],
            glue([r[0], m[1]], [(-o, 32), (32, 96)]),
            glue([m[1], r[1], m[2]], [(32, 32), (32 - o, 32), (64, 64)]),
            glue([m[2], r[2], m[3]], [(64, 64), (64 - o, 32), (96, 32)]),
            glue([m[3], r[3]], [(96, 96), (96 - o, 32)]),
        ]
        for t in range(5):
            cols = slice(zz * 640 + t * 128, zz * 640 + t * 128 + 128)
            out[:, cols] = (gate[:, cols] * (tiles[t] + bias[:, cols])).astype(BF16)

    wait_bytes(stage.at[pl.ds(0, 38)], send_sem)
    for dz in range(1, 8):
        wait_bytes(lbuf.at[xl, z], l_send.at[dz])
    wait_bytes(lbuf.at[xl], l_send.at[0])

    @pl.when(xh != c)
    def _():
        wait_bytes(wsrc, wx_send.at[0])

    for dz in range(8):
        zs = (z - dz + 8) % 8
        for dx in (1, 2, 3):
            @pl.when((x + dx) % 4 < 3)
            def _(dx=dx):
                wait_bytes(recv_a.at[zs, :, pl.ds(0, 2)], kv_send.at[dx - 1, dz])

        @pl.when(zs // 3 != x)
        def _():
            wait_bytes(recv_a.at[zs, :, 2], q_send.at[dz])
    for dr in range(4):
        if dr == 0:
            @pl.when(x != 3)
            def _():
                wait_bytes(bsrc, kvb_send.at[0])
                wait_bytes(qsrc_b, qb_send.at[0])
        else:
            wait_bytes(bsrc, kvb_send.at[dr])

    @pl.when(x < 3)
    def _():
        for dz in DZ:
            zs = (z - dz + 8) % 8
            wait_bytes(kv.at[:, c, zs // 4, zs % 4], sib_send.at[dz])

    @pl.when(x == 3)
    def _():
        for dr in range(4):
            wait_bytes(kv.at[:, c, :, (z - dr + 4) % 4], sib_send.at[dr])

    for s in (1, 2, 3, 4):
        for cp in w_copies(s):
            cp.wait_send()
    for k, zb in w_order():
        wait_bytes(wbuf.at[c, zb], ws_send.at[k])
    for l in range(2):
        for zi in range(3):
            zt, xd, here = c_place(zi, l)

            @pl.when((zi < n_zi) & jnp.logical_not(here))
            def _(l=l, zi=zi):
                wait_bytes(att.at[zi, l], c_send.at[l, zi])
        for dx in (1, 2, 3):
            wait_bytes(att_t.at[l, x], r_send.at[l, 0, dx - 1])
            wait_bytes(att_t.at[l, 5 + x], r_send.at[l, 1, dx - 1])

            @pl.when(xl == l)
            def _(l=l, dx=dx):
                wait_bytes(att_t.at[l, xh * 5 + 4], r_send.at[l, 2, dx - 1])
        for g in range(2):
            for dy in (1, 2, 3):
                rs_copy(l, g, dy).wait_send()
        for a in range(2):
            @pl.when(f_place(l, a) != x)
            def _(l=l, a=a):
                wait_bytes(rsum.at[l, a], f_send.at[l, a])


VM = pl.BlockSpec(memory_space=pltpu.VMEM)
SM = pl.BlockSpec(memory_space=pltpu.SMEM)
DMA = pltpu.SemaphoreType.DMA
LIMIT = 48 * 2**20
B_AT = 3
B_FWD = 5
W1_AT = 2
W2_AT = 8


def body(queries, keys, values, block_lists, block_counts, out_weight, out_bias, out_gate):
    vm = pltpu.VMEM
    return pl.pallas_call(
        mega_kernel,
        out_shape=jax.ShapeDtypeStruct((16, 5120), BF16),
        in_specs=[VM, VM, VM, VM, SM, VM, VM, VM],
        out_specs=VM,
        scratch_shapes=[
            vm((40, 3, 16, 128), BF16),
            vm((8, 4, 3, 16, 128), BF16),
            vm((2, 4, 3, 16, 128), BF16),
            vm((4, 2, 2, 4, 4, 2, 16, 128), BF16),
            vm((4, 3, 4, 16, 128), BF16),
            vm((2, 8, 1, 128), jnp.int32),
            pltpu.SMEM((2, 8, 1, 128), jnp.int32),
            vm((SLOTS * 128, 128), BF16),
            vm((SLOTS * 128, 128), BF16),
            vm((SLOTS, 128, 128), F32),
            vm((128, SLOTS * 128), BF16),
            vm((3, 2, 128, 128), BF16),
            vm((2, 10, 128, 128), BF16),
            vm((800, 128), BF16),
            vm((2, 8, 800, 128), BF16),
            vm((128, 1280), BF16),
            vm((2, 640, 256), BF16),
            vm((2, 4, 5, 2, 16, 256), BF16),
            vm((2, 4, 5, 2, 16, 256), BF16),
            vm((2, 2, 5, 16, 256), BF16),
            vm((4, 5, 16, 256), BF16),
            DMA, DMA((8,)), DMA((1,)), DMA((3, 8)), DMA((8,)), DMA((4,)), DMA((4,)),
            DMA((8,)), DMA((8,)), DMA((8,)), DMA((1,)), DMA((1,)), DMA((8,)), DMA((8,)), DMA((1,)),
            DMA((1,)), DMA((1,)), DMA((2, 4)), DMA((2, 4)), DMA((8,)), DMA((8,)),
            DMA((2, 3)), DMA((2, 3)), DMA((2, 3, 3)), DMA((2, 10)), DMA((2, 2, 3)), DMA((2, 2)),
            DMA((2, 2)), DMA((4,)),
        ],
        compiler_params=pltpu.CompilerParams(
            collective_id=0, has_side_effects=True, vmem_limit_bytes=LIMIT
        ),
        name="block_sparse_attention",
    )(queries, keys, values, block_lists, block_counts, out_weight,
      out_bias.reshape(1, -1), out_gate.reshape(1, -1))


def solution(mesh):
    in_specs = (
        P(("blk", "uly"), None),
        P(("blk", "uly"), None),
        P(("blk", "uly"), None),
        P("blk", None),
        P("blk"),
        P("uly", "blk"),
        P(),
        P(),
    )
    out_specs = P(("blk", "uly"), None)
    return jax.shard_map(body, mesh=mesh, in_specs=in_specs, out_specs=out_specs, check_vma=False)
```

```python
import functools

import jax
import jax.numpy as jnp
from jax import lax
from jax.experimental import pallas as pl
from jax.experimental.pallas import tpu as pltpu
from jax.sharding import PartitionSpec as P

MESH = pl.DeviceIdType.MESH
HEAD_DIM = 128
SLOTS = 12
FEWEST = 4
DZ = (0, 1, 7, 2, 6, 3, 5, 4)
BF16 = jnp.bfloat16
F32 = jnp.float32


def coords():
    b = lax.axis_index("blk")
    u = lax.axis_index("uly")
    return (u % 2) * 2 + (b // 2) % 2, u // 2, b // 4, b % 2


def dev(x, y, z, c):
    return (z * 4 + (x % 2) * 2 + c, y * 2 + x // 2)


def wait_bytes(ref, sem):
    pltpu.make_async_copy(ref, ref, sem).wait()


def remote(src, dst, send, recv, device):
    return pltpu.make_async_remote_copy(
        src, dst, send, recv, device_id=device, device_id_type=MESH
    )


def mega_kernel(
    q_ref, k_ref, v_ref, lists_ref, counts_ref, w_ref, bias, gate, out,
    lin, bin_, gin, recv_a, recv_b, recv_q, kv, qbuf, lbuf, lsm,
    sc, att, att_t, wbuf, acat, psend, precv, rsum, rrecv,
    a_send, b_send, a_sem, b_sem, kv_send, kv_sem,
    sib_send, sib_sem, q_send, q_sem, l_send, l_recv, l_sem,
    wx_send, wx_recv, w_send, w_recv, ws_send, ws_recv,
    c_send, c_recv, r_send, r_recv, rs_send, rs_recv, f_send, f_recv, in_sem,
):
    x, y, z, c = coords()
    half = z // 4
    row = z % 4
    xh = x // 2
    xl = x % 2
    double = row == y
    z_base = jnp.where(double, 4 * (x % 2), 2 * x)
    n_zi = jnp.where(double, 4, 2)
    j_mine = jnp.where(double & (x >= 2), 4, row)

    peers = [
        dev(x, (y + dy) % 4, (z + dz) % 8, c)
        for dz in range(8) for dy in range(4) if (dy, dz) != (0, 0)
    ]
    peers += [dev((x + dx) % 4, y, (z + dz) % 8, c) for dz in range(8) for dx in (1, 2, 3)]
    peers += [dev(x, y, z, 1 - c), dev((x + 2) % 4, y, z, 1 - c)]
    bar = pltpu.get_barrier_semaphore()
    for d in peers:
        pl.semaphore_signal(bar, inc=1, device_id=d, device_id_type=MESH)
    loads = [
        pltpu.make_async_copy(src, dst, in_sem.at[i])
        for i, (src, dst) in enumerate(((lists_ref, lin), (bias, bin_), (gate, gin)))
    ]
    for cp in loads:
        cp.start()
    loads[0].wait()
    lbuf[xl, z] = jnp.full((1, 128), counts_ref[0], jnp.int32)
    lbuf[xl, z, :, 0:SLOTS] = lin[...]
    pl.semaphore_wait(bar, len(peers))

    ruler = kv.reshape(512, 16, 128)

    def wait_blocks(n, sem):
        wait_bytes(ruler.at[pl.ds(0, n)], sem)

    def lists_z():
        for dz in range(1, 8):
            remote(lbuf.at[xl, z], lbuf.at[xl, z], l_send.at[dz], l_recv.at[dz],
                   dev(x, y, (z + dz) % 8, c)).start()

    def stage1(dz):
        zd = (z + dz) % 8
        hd = zd // 4
        rd = zd % 4

        def go(head, yd, here, *refs):
            dst, dst_q, send, recv = refs
            cols = pl.ds(pl.multiple_of(head * HEAD_DIM, HEAD_DIM), HEAD_DIM)
            for src, to in ((k_ref, dst.at[z, y, 0]), (v_ref, dst.at[z, y, 1]), (q_ref, dst_q)):
                if here:
                    pltpu.make_async_copy(src.at[:, cols], to, recv).start()
                else:
                    remote(src.at[:, cols], to, send, recv, dev(x, yd, zd, c)).start()

        def loop(dy, _, here=False):
            yd = (y + dy) % 4
            go(yd * 10 + hd * 5 + rd, yd, here, recv_a, recv_q.at[0, z, y], a_send, a_sem.at[dz])
            return 0

        if dz == 0:
            loop(0, 0, True)
        lax.fori_loop(1 if dz == 0 else 0, 4, loop, 0)
        fifth = functools.partial(go, rd * 10 + hd * 5 + 4, rd)
        refs = (recv_b, recv_q.at[1, z, y], b_send, b_sem.at[dz])
        if dz == 0:
            @pl.when(double)
            def _():
                fifth(True, *refs)

            @pl.when(jnp.logical_not(double))
            def _():
                fifth(False, *refs)
        else:
            fifth(False, *refs)

    slot = (0, 2, 4, 6, 7, 5, 3, 1)

    def w_exchange():
        @pl.when(xh == c)
        def _():
            pltpu.make_async_copy(w_ref, wbuf.at[c, 0], wx_recv.at[0]).start()

        @pl.when(xh != c)
        def _():
            remote(w_ref, wbuf.at[xh, 0], wx_send.at[0], wx_recv.at[0],
                   dev((x + 2) % 4, y, z, 1 - c)).start()

    def w_part(d, s, way):
        at = wbuf.at[c, slot[d % 8]]
        return at if s < 4 else at.at[pl.ds(80 * way, 80)]

    def w_copies(s):
        got = []
        for way, sign in ((0, 1), (1, -1)):
            got.append(remote(
                w_part(-sign * (s - 1), s, way), w_part(-sign * s, s, way),
                w_send.at[way, s - 1], w_recv.at[way, s - 1],
                dev(x, y, (z + sign + 8) % 8, c),
            ))
        return got

    def w_sib(d):
        at = wbuf.at[c, slot[d]]
        return remote(at, at, ws_send.at[d], ws_recv.at[d], dev(x, y, z, 1 - c))

    def w_start(s):
        if s == 1:
            wait_bytes(wbuf.at[c, 0], wx_recv.at[0])
        else:
            for way, sign in ((0, 1), (1, -1)):
                wait_bytes(w_part(-sign * (s - 1), s - 1, way), w_recv.at[way, s - 2])
        if s < 5:
            for cp in w_copies(s):
                cp.start()
        for d in {1: (0,), 2: (7, 1), 3: (6, 2), 4: (5, 3), 5: (4,)}[s]:
            w_sib(d).start()

    def forward(dz):
        zs = (z - dz + 8) % 8
        wait_blocks(12, a_sem.at[dz])

        @pl.when(double)
        def _():
            wait_blocks(12, b_sem.at[dz])

        dst = kv.at[x, c, zs]
        for dx in (2, 1, 3, 0):
            xd = (x + dx) % 4
            second = double & (xd >= 2)
            for take, src in ((jnp.logical_not(second), recv_a), (second, recv_b)):
                src = src.at[zs]

                @pl.when(take)
                def _(dx=dx, xd=xd, src=src):
                    if dx == 0:
                        pltpu.make_async_copy(src, dst, kv_sem.at[dz]).start()
                    else:
                        remote(src, dst, kv_send.at[dx - 1, dz], kv_sem.at[dz],
                               dev(xd, y, z, c)).start()

        xq = jnp.where(double, zs // 4, zs // 2)
        dst_q = qbuf.at[x, jnp.where(double, zs % 4, zs % 2)]

        def go(src, xd, k):
            @pl.when(xd == x)
            def _():
                pltpu.make_async_copy(src, dst_q, q_sem.at[0]).start()

            @pl.when(xd != x)
            def _():
                remote(src, dst_q, q_send.at[k, dz], q_sem.at[0], dev(xd, y, z, c)).start()

        go(recv_q.at[0, zs], xq, 0)

        @pl.when(double)
        def _():
            go(recv_q.at[1, zs], 2 + zs // 4, 1)

    def to_sibling(dz):
        got = kv.at[:, c, (z - dz + 8) % 8]
        wait_bytes(got, kv_sem.at[dz])
        remote(got, got, sib_send.at[dz], sib_sem.at[dz], dev(x, y, z, 1 - c)).start()

    def forward_lists():
        for dz in range(1, 8):
            wait_bytes(lbuf.at[xl, (z - dz + 8) % 8], l_recv.at[dz])
        remote(lbuf.at[xl], lbuf.at[xl], l_send.at[0], l_recv.at[0],
               dev(xh * 2 + 1 - xl, y, z, c)).start()

    def place_lists():
        wait_bytes(lbuf.at[1 - xl], l_recv.at[0])
        cp = pltpu.make_async_copy(lbuf, lsm, l_sem.at[0])
        cp.start()
        cp.wait()

    act = {
        "S": stage1, "F": forward, "T": to_sibling, "W": w_start,
        "X": w_exchange, "L": lists_z, "l": forward_lists,
    }
    for step in SEQ:
        act[step[0]](*[int(n) for n in step[1:]])

    place_lists()

    @pl.when(double)
    def _():
        wait_bytes(qbuf, q_sem.at[0])

    @pl.when(jnp.logical_not(double))
    def _():
        wait_bytes(qbuf.at[:, pl.ds(0, 2)], q_sem.at[0])

    for dz in DZ:
        wait_bytes(kv.at[:, 1 - c, (z - dz + 8) % 8], sib_sem.at[dz])

    scale = float(HEAD_DIM ** -0.5 * 1.4426950408889634)
    h_mine = half * 5 + j_mine
    slot_mine = jnp.where(j_mine < 4, half, 2)

    def c_place(zi, l):
        zt = (z_base + zi) % 8
        xd = jnp.where(j_mine < 4, row, half * 2 + l)
        return zt, xd, (zt == z) & (xd == x)

    def item_scores(zi, l, n):
        zq = (z_base + zi) % 8
        count = lsm[l, zq, 0, SLOTS]
        q = jnp.concatenate(
            [qbuf[l, zi].reshape(64, 128), qbuf[l + 2, zi].reshape(64, 128)], axis=0
        )
        blocks = [lsm[l, zq, 0, s] for s in range(SLOTS)]
        top = None
        for s in range(SLOTS):
            part = lax.dot_general(
                q, rows_of(blocks[s], 0), (((1,), (1,)), ((), ())), preferred_element_type=F32
            )
            if s >= FEWEST:
                part = jnp.where(s < count, part, -1e30)
            sc[n, s] = part
            top = part if top is None else jnp.maximum(top, part)
        return blocks, jnp.max(top, axis=1, keepdims=True)

    def item_values(zi, l, n, blocks, top):
        den = jnp.zeros((128, 128), F32)
        mixed = jnp.zeros((128, 128), F32)
        for s in range(0, SLOTS, 2):
            pair = []
            for t in (s, s + 1):
                p = jnp.exp2((sc[n, t] - top) * scale)
                den = den + p
                pair.append(p.astype(BF16))
            mixed = mixed + jnp.dot(
                jnp.concatenate(pair, axis=1),
                jnp.concatenate([rows_of(blocks[s], 1), rows_of(blocks[s + 1], 1)], axis=0),
                preferred_element_type=F32,
            )
        den = jnp.sum(den, axis=1, keepdims=True)
        att[zi, l] = (mixed / den).astype(BF16)

    def rows_of(kb, which):
        return jnp.concatenate(
            [kv[(kb // 2) % 2 + 2 * a, kb % 2, kb // 4, :, which].reshape(64, 128) for a in range(2)],
            axis=0,
        )

    def item_send(zi, l):
        zt, xd, here = c_place(zi, l)
        src = att.at[zi, l]
        dst = att_t.at[l, h_mine]
        sem = c_recv.at[l, slot_mine]

        @pl.when(here)
        def _():
            pltpu.make_async_copy(src, dst, sem).start()

        @pl.when(jnp.logical_not(here))
        def _():
            remote(src, dst, c_send.at[l, zi], sem, dev(xd, y, zt, c)).start()

    def items(l):
        def step(i, _):
            first = item_scores(2 * i, l, 0)
            second = item_scores(2 * i + 1, l, 1)
            item_values(2 * i, l, 0, *first)
            item_values(2 * i + 1, l, 1, *second)
            item_send(2 * i, l)
            item_send(2 * i + 1, l)
            return 0

        lax.fori_loop(0, n_zi // 2, step, 0)

    def relay_one(l, h, k):
        got = att_t.at[l, h]
        wait_bytes(got, c_recv.at[l, k])
        for dx in (2, 1, 3):
            remote(got, got, r_send.at[l, k, dx - 1], r_recv.at[l, h],
                   dev((x + dx) % 4, y, z, c)).start()

    def relay(l, k):
        if k < 2:
            relay_one(l, 5 * k + x, k)
        else:
            @pl.when(xl == l)
            def _():
                relay_one(l, xh * 5 + 4, 2)

    def relayed(l):
        for h in range(10):
            source = h % 5 if h % 5 < 4 else (h // 5) * 2 + l

            @pl.when(x != source)
            def _(h=h):
                wait_bytes(att_t.at[l, h], r_recv.at[l, h])

            acat[l, :, h * 128 : h * 128 + 128] = att_t[l, h]

    def rs_copy(l, t, dy):
        yd = (y + dy) % 4
        return remote(psend.at[l, yd, t], precv.at[l, y, t], rs_send.at[l, t, dy - 1],
                      rs_recv.at[l, t], dev(x, yd, z, c))

    def from_sibling(s):
        for d in {1: (0,), 2: (7, 1), 3: (6, 2), 4: (5, 3), 5: (4,)}[s]:
            wait_bytes(wbuf.at[1 - c, slot[d]], ws_recv.at[d])

    def project(l, t):
        r = None
        for k in range(2):
            w = wbuf.reshape(2, 1280, 640)[k, 256 * t : 256 * t + 256]
            got = lax.dot_general(
                acat[l, :, 640 * k : 640 * k + 640], w, (((1,), (1,)), ((), ())),
                preferred_element_type=F32,
            )
            r = got if r is None else r + got
        r = r.astype(BF16).reshape(2, 4, 16, 256)
        for yy in range(4):
            for a in range(2):
                psend[l, yy, t, a] = r[a, yy]
        for dy in (2, 1, 3):
            rs_copy(l, t, dy).start()

    def f_place(l, a):
        return a * 2 + l

    def reduce(l):
        for t in (0, 1, 2, 3, 4):
            wait_bytes(precv.at[l, pl.ds(0, 3), t], rs_recv.at[l, t])
            total = psend[l, y, t].astype(F32)
            for d in (1, 2, 3):
                total = total + precv[l, (y + d) % 4, t].astype(F32)
            total = total.astype(BF16)
            for a in range(2):
                rsum[l, a, t] = total[a]
        for a in range(2):
            xd = f_place(l, a)

            @pl.when(xd == x)
            def _(a=a):
                rrecv[x] = rsum[l, a]

            @pl.when(xd != x)
            def _(a=a, xd=xd):
                remote(rsum.at[l, a], rrecv.at[x], f_send.at[l, a], f_recv.at[x],
                       dev(xd, y, z, c)).start()

    act = {
        "I": items, "R": relay, "G": relayed, "P": project, "D": reduce, "W": w_start,
        "V": from_sibling,
    }
    for step in SEQ_OUT:
        act[step[0]](*[int(n) for n in step[1:]])

    for d in (1, 2, 3):
        xs = (x + d) % 4
        wait_bytes(rrecv.at[xs], f_recv.at[xs])
    loads[1].wait()
    loads[2].wait()
    quarters = [
        jnp.concatenate([rrecv[xs, t].astype(F32) for t in range(5)], axis=1) for xs in (0, 2, 1, 3)
    ]
    for d in range(8):
        lo = 160 * slot[d]
        made = jnp.concatenate([part[:, lo : lo + 160] for part in quarters], axis=1)
        cols = pl.ds(pl.multiple_of((z + d) % 8 * 640, 128), 640)
        out[:, cols] = (gin[:, cols] * (made + bin_[:, cols])).astype(BF16)

    wait_blocks(31 * 3, a_send)
    for take, n in ((double, 7), (jnp.logical_not(double), 8)):
        @pl.when(take)
        def _(n=n):
            wait_blocks(n * 3, b_send)
    for dz in range(1, 8):
        wait_bytes(lbuf.at[xl, z], l_send.at[dz])
    wait_bytes(lbuf.at[xl], l_send.at[0])

    @pl.when(xh != c)
    def _():
        wait_bytes(w_ref, wx_send.at[0])

    for dz in range(8):
        zs = (z - dz + 8) % 8
        for dx in (1, 2, 3):
            wait_bytes(kv.at[x, c, zs], kv_send.at[dx - 1, dz])
        xq = jnp.where(double, zs // 4, zs // 2)

        @pl.when(xq != x)
        def _():
            wait_bytes(recv_q.at[0, zs], q_send.at[0, dz])

        @pl.when(double & (2 + zs // 4 != x))
        def _():
            wait_bytes(recv_q.at[1, zs], q_send.at[1, dz])

        wait_bytes(kv.at[:, c, zs], sib_send.at[dz])

    for s in (1, 2, 3, 4):
        for cp in w_copies(s):
            cp.wait_send()
    for d in range(8):
        w_sib(d).wait_send()
    for l in range(2):
        for zi in range(4):
            zt, xd, here = c_place(zi, l)

            @pl.when((zi < n_zi) & jnp.logical_not(here))
            def _(l=l, zi=zi):
                wait_bytes(att.at[zi, l], c_send.at[l, zi])
        for dx in (1, 2, 3):
            wait_bytes(att_t.at[l, x], r_send.at[l, 0, dx - 1])
            wait_bytes(att_t.at[l, 5 + x], r_send.at[l, 1, dx - 1])

            @pl.when(xl == l)
            def _(l=l, dx=dx):
                wait_bytes(att_t.at[l, xh * 5 + 4], r_send.at[l, 2, dx - 1])
        for t in range(5):
            for dy in (1, 2, 3):
                rs_copy(l, t, dy).wait_send()
        for a in range(2):
            @pl.when(f_place(l, a) != x)
            def _(l=l, a=a):
                wait_bytes(rsum.at[l, a], f_send.at[l, a])


VM = pl.BlockSpec(memory_space=pltpu.VMEM)
SM = pl.BlockSpec(memory_space=pltpu.SMEM)
DMA = pltpu.SemaphoreType.DMA
LIMIT = 63 * 2**20
HBM = pl.BlockSpec(memory_space=pl.ANY)
SEQ = (
    "X", "L", "S0", "S1", "S7", "S2", "S6", "S3", "S5", "S4", "F0", "F1", "F7", "T0", "W1", "F2",
    "F6", "T1", "T7", "F3", "F5", "T2", "T6", "F4", "W2", "l", "T3", "T5", "T4",
)
SEQ_OUT = (
    "I0", "W3", "I1", "R00", "R01", "R02", "W4", "R10", "R11", "R12", "G0", "V1", "V2", "V3",
    "P00", "P01", "P02", "V4", "P03", "W5", "V5", "P04", "G1", "P10", "P11", "P12", "P13", "P14",
    "D0", "D1",
)


def body(queries, keys, values, block_lists, block_counts, out_weight, out_bias, out_gate):
    vm = pltpu.VMEM
    return pl.pallas_call(
        mega_kernel,
        out_shape=jax.ShapeDtypeStruct((16, 5120), BF16),
        in_specs=[HBM, HBM, HBM, HBM, SM, HBM, HBM, HBM],
        out_specs=VM,
        scratch_shapes=[
            vm((1, SLOTS), jnp.int32),
            vm((1, 5120), F32),
            vm((1, 5120), F32),
            vm((8, 4, 2, 16, 128), BF16),
            vm((8, 4, 2, 16, 128), BF16),
            vm((2, 8, 4, 16, 128), BF16),
            vm((4, 2, 8, 4, 2, 16, 128), BF16),
            vm((4, 4, 4, 16, 128), BF16),
            vm((2, 8, 1, 128), jnp.int32),
            pltpu.SMEM((2, 8, 1, 128), jnp.int32),
            vm((2, SLOTS, 128, 128), F32),
            vm((4, 2, 128, 128), BF16),
            vm((2, 10, 128, 128), BF16),
            vm((2, 8, 160, 640), BF16),
            vm((2, 128, 1280), BF16),
            vm((2, 4, 5, 2, 16, 256), BF16),
            vm((2, 4, 5, 2, 16, 256), BF16),
            vm((2, 2, 5, 16, 256), BF16),
            vm((4, 5, 16, 256), BF16),
            DMA, DMA, DMA((8,)), DMA((8,)), DMA((3, 8)), DMA((8,)),
            DMA((8,)), DMA((8,)), DMA((2, 8)), DMA((1,)), DMA((8,)), DMA((8,)), DMA((1,)),
            DMA((1,)), DMA((1,)), DMA((2, 4)), DMA((2, 4)), DMA((8,)), DMA((8,)),
            DMA((2, 4)), DMA((2, 3)), DMA((2, 3, 3)), DMA((2, 10)), DMA((2, 5, 3)), DMA((2, 5)),
            DMA((2, 2)), DMA((4,)), DMA((3,)),
        ],
        compiler_params=pltpu.CompilerParams(
            collective_id=0, has_side_effects=True, vmem_limit_bytes=LIMIT
        ),
        name="block_sparse_attention",
    )(queries, keys, values, block_lists, block_counts, out_weight.T,
      out_bias.reshape(1, -1), out_gate.reshape(1, -1))


def solution(mesh):
    in_specs = (
        P(("blk", "uly"), None),
        P(("blk", "uly"), None),
        P(("blk", "uly"), None),
        P("blk", None),
        P("blk"),
        P("uly", "blk"),
        P(),
        P(),
    )
    out_specs = P(("blk", "uly"), None)
    return jax.shard_map(body, mesh=mesh, in_specs=in_specs, out_specs=out_specs, check_vma=False)
```

```python
import functools

import jax
import jax.numpy as jnp
from jax import lax
from jax.experimental import pallas as pl
from jax.experimental.pallas import tpu as pltpu
from jax.sharding import PartitionSpec as P

MESH = pl.DeviceIdType.MESH
HEAD_DIM = 128
SLOTS = 12
FEWEST = 4
DZ = (0, 1, 7, 2, 6, 3, 5, 4)
BF16 = jnp.bfloat16
F32 = jnp.float32


def coords():
    b = lax.axis_index("blk")
    u = lax.axis_index("uly")
    return (u % 2) * 2 + (b // 2) % 2, u // 2, b // 4, b % 2


def dev(x, y, z, c):
    return (z * 4 + (x % 2) * 2 + c, y * 2 + x // 2)


def wait_bytes(ref, sem):
    pltpu.make_async_copy(ref, ref, sem).wait()


def remote(src, dst, send, recv, device):
    return pltpu.make_async_remote_copy(
        src, dst, send, recv, device_id=device, device_id_type=MESH
    )


def mega_kernel(
    q_ref, k_ref, v_ref, lists_ref, counts_ref, w_ref, bias, gate, out,
    lin, bin_, gin, recv_a, recv_b, recv_q, kv, qbuf, lbuf, lsm,
    sc, att, att_t, wbuf, acat, psend, precv, rsum, rrecv,
    a_send, b_send, a_sem, b_sem, kv_send, kv_sem,
    sib_send, sib_sem, q_send, q_sem, l_send, l_recv, l_sem,
    wx_send, wx_recv, w_send, w_recv, ws_send, ws_recv,
    c_send, c_recv, r_send, r_recv, rs_send, rs_recv, f_send, f_recv, in_sem,
):
    x, y, z, c = coords()
    half = z // 4
    row = z % 4
    xh = x // 2
    xl = x % 2
    double = row == y
    z_base = jnp.where(double, 4 * (x % 2), 2 * x)
    n_zi = jnp.where(double, 4, 2)
    j_mine = jnp.where(double & (x >= 2), 4, row)

    peers = [
        dev(x, (y + dy) % 4, (z + dz) % 8, c)
        for dz in range(8) for dy in range(4) if (dy, dz) != (0, 0)
    ]
    peers += [dev((x + dx) % 4, y, (z + dz) % 8, c) for dz in range(8) for dx in (1, 2, 3)]
    peers += [dev(x, y, z, 1 - c), dev((x + 2) % 4, y, z, 1 - c)]
    bar = pltpu.get_barrier_semaphore()
    for d in peers:
        pl.semaphore_signal(bar, inc=1, device_id=d, device_id_type=MESH)
    loads = [
        pltpu.make_async_copy(src, dst, in_sem.at[i])
        for i, (src, dst) in enumerate(((lists_ref, lin), (bias, bin_), (gate, gin)))
    ]
    for cp in loads:
        cp.start()
    loads[0].wait()
    lbuf[xl, z] = jnp.full((1, 128), counts_ref[0], jnp.int32)
    lbuf[xl, z, :, 0:SLOTS] = lin[...]
    pl.semaphore_wait(bar, len(peers))

    ruler = kv.reshape(512, 16, 128)

    def wait_blocks(n, sem):
        wait_bytes(ruler.at[pl.ds(0, n)], sem)

    def lists_z():
        for dz in range(1, 8):
            remote(lbuf.at[xl, z], lbuf.at[xl, z], l_send.at[dz], l_recv.at[dz],
                   dev(x, y, (z + dz) % 8, c)).start()

    def stage1(dz):
        zd = (z + dz) % 8
        hd = zd // 4
        rd = zd % 4

        def go(head, yd, here, *refs):
            dst, dst_q, send, recv = refs
            cols = pl.ds(pl.multiple_of(head * HEAD_DIM, HEAD_DIM), HEAD_DIM)
            for src, to in ((k_ref, dst.at[z, y, 0]), (v_ref, dst.at[z, y, 1]), (q_ref, dst_q)):
                if here:
                    pltpu.make_async_copy(src.at[:, cols], to, recv).start()
                else:
                    remote(src.at[:, cols], to, send, recv, dev(x, yd, zd, c)).start()

        def loop(dy, _, here=False):
            yd = (y + dy) % 4
            go(yd * 10 + hd * 5 + rd, yd, here, recv_a, recv_q.at[0, z, y], a_send, a_sem.at[dz])
            return 0

        if dz == 0:
            loop(0, 0, True)
        lax.fori_loop(1 if dz == 0 else 0, 4, loop, 0)
        fifth = functools.partial(go, rd * 10 + hd * 5 + 4, rd)
        refs = (recv_b, recv_q.at[1, z, y], b_send, b_sem.at[dz])
        if dz == 0:
            @pl.when(double)
            def _():
                fifth(True, *refs)

            @pl.when(jnp.logical_not(double))
            def _():
                fifth(False, *refs)
        else:
            fifth(False, *refs)

    slot = (0, 2, 4, 6, 7, 5, 3, 1)

    def w_exchange():
        @pl.when(xh == c)
        def _():
            pltpu.make_async_copy(w_ref, wbuf.at[c, 0], wx_recv.at[0]).start()

        @pl.when(xh != c)
        def _():
            remote(w_ref, wbuf.at[xh, 0], wx_send.at[0], wx_recv.at[0],
                   dev((x + 2) % 4, y, z, 1 - c)).start()

    def w_part(d, s, way):
        at = wbuf.at[c, slot[d % 8]]
        return at if s < 4 else at.at[pl.ds(80 * way, 80)]

    def w_copies(s):
        got = []
        for way, sign in ((0, 1), (1, -1)):
            got.append(remote(
                w_part(-sign * (s - 1), s, way), w_part(-sign * s, s, way),
                w_send.at[way, s - 1], w_recv.at[way, s - 1],
                dev(x, y, (z + sign + 8) % 8, c),
            ))
        return got

    def w_sib(d):
        at = wbuf.at[c, slot[d]]
        return remote(at, at, ws_send.at[d], ws_recv.at[d], dev(x, y, z, 1 - c))

    def w_start(s):
        if s == 1:
            wait_bytes(wbuf.at[c, 0], wx_recv.at[0])
        else:
            for way, sign in ((0, 1), (1, -1)):
                wait_bytes(w_part(-sign * (s - 1), s - 1, way), w_recv.at[way, s - 2])
        if s < 5:
            for cp in w_copies(s):
                cp.start()
        for d in {1: (0,), 2: (7, 1), 3: (6, 2), 4: (5, 3), 5: (4,)}[s]:
            w_sib(d).start()

    def forward(dz):
        zs = (z - dz + 8) % 8
        wait_blocks(12, a_sem.at[dz])

        @pl.when(double)
        def _():
            wait_blocks(12, b_sem.at[dz])

        dst = kv.at[x, c, zs]
        for dx in (2, 1, 3, 0):
            xd = (x + dx) % 4
            second = double & (xd >= 2)
            for take, src in ((jnp.logical_not(second), recv_a), (second, recv_b)):
                src = src.at[zs]

                @pl.when(take)
                def _(dx=dx, xd=xd, src=src):
                    if dx == 0:
                        pltpu.make_async_copy(src, dst, kv_sem.at[dz]).start()
                    else:
                        remote(src, dst, kv_send.at[dx - 1, dz], kv_sem.at[dz],
                               dev(xd, y, z, c)).start()

        xq = jnp.where(double, zs // 4, zs // 2)
        dst_q = qbuf.at[x, jnp.where(double, zs % 4, zs % 2)]

        def go(src, xd, k):
            @pl.when(xd == x)
            def _():
                pltpu.make_async_copy(src, dst_q, q_sem.at[0]).start()

            @pl.when(xd != x)
            def _():
                remote(src, dst_q, q_send.at[k, dz], q_sem.at[0], dev(xd, y, z, c)).start()

        go(recv_q.at[0, zs], xq, 0)

        @pl.when(double)
        def _():
            go(recv_q.at[1, zs], 2 + zs // 4, 1)

    def to_sibling(dz):
        got = kv.at[:, c, (z - dz + 8) % 8]
        wait_bytes(got, kv_sem.at[dz])
        remote(got, got, sib_send.at[dz], sib_sem.at[dz], dev(x, y, z, 1 - c)).start()

    def forward_lists():
        for dz in range(1, 8):
            wait_bytes(lbuf.at[xl, (z - dz + 8) % 8], l_recv.at[dz])
        remote(lbuf.at[xl], lbuf.at[xl], l_send.at[0], l_recv.at[0],
               dev(xh * 2 + 1 - xl, y, z, c)).start()

    def place_lists():
        wait_bytes(lbuf.at[1 - xl], l_recv.at[0])
        cp = pltpu.make_async_copy(lbuf, lsm, l_sem.at[0])
        cp.start()
        cp.wait()

    act = {
        "S": stage1, "F": forward, "T": to_sibling, "W": w_start,
        "X": w_exchange, "L": lists_z, "l": forward_lists,
    }
    for step in SEQ:
        act[step[0]](*[int(n) for n in step[1:]])

    place_lists()

    @pl.when(double)
    def _():
        wait_bytes(qbuf, q_sem.at[0])

    @pl.when(jnp.logical_not(double))
    def _():
        wait_bytes(qbuf.at[:, pl.ds(0, 2)], q_sem.at[0])

    for dz in DZ:
        wait_bytes(kv.at[:, 1 - c, (z - dz + 8) % 8], sib_sem.at[dz])

    scale = float(HEAD_DIM ** -0.5 * 1.4426950408889634)
    h_mine = half * 5 + j_mine
    slot_mine = jnp.where(j_mine < 4, half, 2)

    def c_place(zi, l):
        zt = (z_base + zi) % 8
        xd = jnp.where(j_mine < 4, (row + 2 * (zt % 2)) % 4, half * 2 + l)
        return zt, xd, (zt == z) & (xd == x)

    def item_scores(zi, l, n):
        zq = (z_base + zi) % 8
        count = lsm[l, zq, 0, SLOTS]
        q = jnp.concatenate(
            [qbuf[l, zi].reshape(64, 128), qbuf[l + 2, zi].reshape(64, 128)], axis=0
        )
        blocks = [lsm[l, zq, 0, s] for s in range(SLOTS)]
        right = lax.broadcasted_iota(jnp.int32, (1, 256), 1) // 128
        top = None
        for s in range(0, SLOTS, 2):
            part = lax.dot_general(
                q, pair_of(blocks, s, 0), (((1,), (1,)), ((), ())), preferred_element_type=F32
            )
            if s >= FEWEST:
                part = jnp.where(right + s < count, part, -1e30)
            sc[n, s // 2] = part
            top = part if top is None else jnp.maximum(top, part)
        return blocks, jnp.max(top, axis=1, keepdims=True)

    def item_values(zi, l, n, blocks, top):
        den = jnp.zeros((128, 256), F32)
        mixed = jnp.zeros((128, 128), F32)
        for s in range(0, SLOTS, 2):
            p = jnp.exp2((sc[n, s // 2] - top) * scale)
            den = den + p
            mixed = mixed + jnp.dot(
                p.astype(BF16), pair_of(blocks, s, 1), preferred_element_type=F32
            )
        den = jnp.sum(den, axis=1, keepdims=True)
        att[zi, l] = (mixed / den).astype(BF16)

    def pair_of(blocks, s, which):
        return jnp.concatenate([rows_of(blocks[s], which), rows_of(blocks[s + 1], which)], axis=0)

    def rows_of(kb, which):
        return jnp.concatenate(
            [kv[(kb // 2) % 2 + 2 * a, kb % 2, kb // 4, :, which].reshape(64, 128) for a in range(2)],
            axis=0,
        )

    def item_send(zi, l):
        zt, xd, here = c_place(zi, l)
        src = att.at[zi, l]
        dst = att_t.at[l, h_mine]
        sem = c_recv.at[l, slot_mine]

        @pl.when(here)
        def _():
            pltpu.make_async_copy(src, dst, sem).start()

        @pl.when(jnp.logical_not(here))
        def _():
            remote(src, dst, c_send.at[l, zi], sem, dev(xd, y, zt, c)).start()

    def items(l):
        def step(i, _):
            first = item_scores(2 * i, l, 0)
            second = item_scores(2 * i + 1, l, 1)
            item_values(2 * i, l, 0, *first)
            item_values(2 * i + 1, l, 1, *second)
            item_send(2 * i, l)
            item_send(2 * i + 1, l)
            return 0

        lax.fori_loop(0, n_zi // 2, step, 0)

    def relay_one(l, h, k):
        got = att_t.at[l, h]
        wait_bytes(got, c_recv.at[l, k])
        for dx in (2, 1, 3):
            remote(got, got, r_send.at[l, k, dx - 1], r_recv.at[l, h],
                   dev((x + dx) % 4, y, z, c)).start()

    def relay(l, k):
        if k < 2:
            relay_one(l, 5 * k + (x + 2 * (z % 2)) % 4, k)
        else:
            @pl.when(xl == l)
            def _():
                relay_one(l, xh * 5 + 4, 2)

    def relayed(l):
        for h in range(10):
            source = (h % 5 + 2 * (z % 2)) % 4 if h % 5 < 4 else (h // 5) * 2 + l

            @pl.when(x != source)
            def _(h=h):
                wait_bytes(att_t.at[l, h], r_recv.at[l, h])

            acat[l, :, h * 128 : h * 128 + 128] = att_t[l, h]

    def rs_copy(l, t, dy):
        yd = (y + dy) % 4
        return remote(psend.at[l, yd, t], precv.at[l, y, t], rs_send.at[l, t, dy - 1],
                      rs_recv.at[l, t], dev(x, yd, z, c))

    def from_sibling(s):
        for d in {1: (0,), 2: (7, 1), 3: (6, 2), 4: (5, 3), 5: (4,)}[s]:
            wait_bytes(wbuf.at[1 - c, slot[d]], ws_recv.at[d])

    def project(l, t):
        r = None
        for k in range(2):
            w = wbuf.reshape(2, 1280, 640)[k, 256 * t : 256 * t + 256]
            got = lax.dot_general(
                acat[l, :, 640 * k : 640 * k + 640], w, (((1,), (1,)), ((), ())),
                preferred_element_type=F32,
            )
            r = got if r is None else r + got
        r = r.astype(BF16).reshape(2, 4, 16, 256)
        for yy in range(4):
            for a in range(2):
                psend[l, yy, t, a] = r[a, yy]
        for dy in (2, 1, 3):
            rs_copy(l, t, dy).start()

    def f_place(l, a):
        return a * 2 + l

    def reduce(l):
        for t in (0, 1, 2, 3, 4):
            wait_bytes(precv.at[l, pl.ds(0, 3), t], rs_recv.at[l, t])
            total = psend[l, y, t].astype(F32)
            for d in (1, 2, 3):
                total = total + precv[l, (y + d) % 4, t].astype(F32)
            total = total.astype(BF16)
            for a in range(2):
                rsum[l, a, t] = total[a]
        for a in range(2):
            xd = f_place(l, a)

            @pl.when(xd == x)
            def _(a=a):
                rrecv[x] = rsum[l, a]

            @pl.when(xd != x)
            def _(a=a, xd=xd):
                remote(rsum.at[l, a], rrecv.at[x], f_send.at[l, a], f_recv.at[x],
                       dev(xd, y, z, c)).start()

    act = {
        "I": items, "R": relay, "G": relayed, "P": project, "D": reduce, "W": w_start,
        "V": from_sibling,
    }
    for step in SEQ_OUT:
        act[step[0]](*[int(n) for n in step[1:]])

    for d in (1, 2, 3):
        xs = (x + d) % 4
        wait_bytes(rrecv.at[xs], f_recv.at[xs])
    loads[1].wait()
    loads[2].wait()
    quarters = [
        jnp.concatenate([rrecv[xs, t].astype(F32) for t in range(5)], axis=1) for xs in (0, 2, 1, 3)
    ]
    for d in range(8):
        lo = 160 * slot[d]
        made = jnp.concatenate([part[:, lo : lo + 160] for part in quarters], axis=1)
        cols = pl.ds(pl.multiple_of((z + d) % 8 * 640, 128), 640)
        out[:, cols] = (gin[:, cols] * (made + bin_[:, cols])).astype(BF16)

    wait_blocks(31 * 3, a_send)
    for take, n in ((double, 7), (jnp.logical_not(double), 8)):
        @pl.when(take)
        def _(n=n):
            wait_blocks(n * 3, b_send)
    for dz in range(1, 8):
        wait_bytes(lbuf.at[xl, z], l_send.at[dz])
    wait_bytes(lbuf.at[xl], l_send.at[0])

    @pl.when(xh != c)
    def _():
        wait_bytes(w_ref, wx_send.at[0])

    for dz in range(8):
        zs = (z - dz + 8) % 8
        for dx in (1, 2, 3):
            wait_bytes(kv.at[x, c, zs], kv_send.at[dx - 1, dz])
        xq = jnp.where(double, zs // 4, zs // 2)

        @pl.when(xq != x)
        def _():
            wait_bytes(recv_q.at[0, zs], q_send.at[0, dz])

        @pl.when(double & (2 + zs // 4 != x))
        def _():
            wait_bytes(recv_q.at[1, zs], q_send.at[1, dz])

        wait_bytes(kv.at[:, c, zs], sib_send.at[dz])

    for s in (1, 2, 3, 4):
        for cp in w_copies(s):
            cp.wait_send()
    for d in range(8):
        w_sib(d).wait_send()
    for l in range(2):
        for zi in range(4):
            zt, xd, here = c_place(zi, l)

            @pl.when((zi < n_zi) & jnp.logical_not(here))
            def _(l=l, zi=zi):
                wait_bytes(att.at[zi, l], c_send.at[l, zi])
        for dx in (1, 2, 3):
            wait_bytes(att_t.at[l, x], r_send.at[l, 0, dx - 1])
            wait_bytes(att_t.at[l, 5 + x], r_send.at[l, 1, dx - 1])

            @pl.when(xl == l)
            def _(l=l, dx=dx):
                wait_bytes(att_t.at[l, xh * 5 + 4], r_send.at[l, 2, dx - 1])
        for t in range(5):
            for dy in (1, 2, 3):
                rs_copy(l, t, dy).wait_send()
        for a in range(2):
            @pl.when(f_place(l, a) != x)
            def _(l=l, a=a):
                wait_bytes(rsum.at[l, a], f_send.at[l, a])


VM = pl.BlockSpec(memory_space=pltpu.VMEM)
SM = pl.BlockSpec(memory_space=pltpu.SMEM)
DMA = pltpu.SemaphoreType.DMA
LIMIT = 63 * 2**20
HBM = pl.BlockSpec(memory_space=pl.ANY)
SEQ = (
    "X", "L", "S0", "S1", "S7", "S2", "S6", "S3", "S5", "S4", "F0", "F1", "F7", "T0", "W1", "F2",
    "F6", "T1", "T7", "F3", "F5", "T2", "T6", "F4", "W2", "l", "T3", "T5", "T4",
)
SEQ_OUT = (
    "I0", "W3", "I1", "R00", "R01", "R02", "W4", "R10", "R11", "R12", "G0", "V1", "V2", "V3",
    "P00", "P01", "P02", "V4", "P03", "W5", "V5", "P04", "G1", "P10", "P11", "P12", "P13", "P14",
    "D0", "D1",
)


def body(queries, keys, values, block_lists, block_counts, out_weight, out_bias, out_gate):
    vm = pltpu.VMEM
    return pl.pallas_call(
        mega_kernel,
        out_shape=jax.ShapeDtypeStruct((16, 5120), BF16),
        in_specs=[HBM, HBM, HBM, HBM, SM, HBM, HBM, HBM],
        out_specs=VM,
        scratch_shapes=[
            vm((1, SLOTS), jnp.int32),
            vm((1, 5120), F32),
            vm((1, 5120), F32),
            vm((8, 4, 2, 16, 128), BF16),
            vm((8, 4, 2, 16, 128), BF16),
            vm((2, 8, 4, 16, 128), BF16),
            vm((4, 2, 8, 4, 2, 16, 128), BF16),
            vm((4, 4, 4, 16, 128), BF16),
            vm((2, 8, 1, 128), jnp.int32),
            pltpu.SMEM((2, 8, 1, 128), jnp.int32),
            vm((2, SLOTS // 2, 128, 256), F32),
            vm((4, 2, 128, 128), BF16),
            vm((2, 10, 128, 128), BF16),
            vm((2, 8, 160, 640), BF16),
            vm((2, 128, 1280), BF16),
            vm((2, 4, 5, 2, 16, 256), BF16),
            vm((2, 4, 5, 2, 16, 256), BF16),
            vm((2, 2, 5, 16, 256), BF16),
            vm((4, 5, 16, 256), BF16),
            DMA, DMA, DMA((8,)), DMA((8,)), DMA((3, 8)), DMA((8,)),
            DMA((8,)), DMA((8,)), DMA((2, 8)), DMA((1,)), DMA((8,)), DMA((8,)), DMA((1,)),
            DMA((1,)), DMA((1,)), DMA((2, 4)), DMA((2, 4)), DMA((8,)), DMA((8,)),
            DMA((2, 4)), DMA((2, 3)), DMA((2, 3, 3)), DMA((2, 10)), DMA((2, 5, 3)), DMA((2, 5)),
            DMA((2, 2)), DMA((4,)), DMA((3,)),
        ],
        compiler_params=pltpu.CompilerParams(
            collective_id=0, has_side_effects=True, vmem_limit_bytes=LIMIT
        ),
        name="block_sparse_attention",
    )(queries, keys, values, block_lists, block_counts, out_weight.T,
      out_bias.reshape(1, -1), out_gate.reshape(1, -1))


def solution(mesh):
    in_specs = (
        P(("blk", "uly"), None),
        P(("blk", "uly"), None),
        P(("blk", "uly"), None),
        P("blk", None),
        P("blk"),
        P("uly", "blk"),
        P(),
        P(),
    )
    out_specs = P(("blk", "uly"), None)
    return jax.shard_map(body, mesh=mesh, in_specs=in_specs, out_specs=out_specs, check_vma=False)
```
